128 devices in a mesh: fsdp: 4 (over z_hi, core), expert: 8 (over y, z_lo), tensor: 4 (over x).
Axes of the slice: x: 4, y: 4, z: 4 (z_hi: 2, z_lo: 2; z = z_hi * 2 + z_lo), core: 2. Of those that a mesh axis runs over, the one named last changes fastest.
Arguments:
- attn_partial: bfloat16 [4, 16384, 7168], P('tensor', ('fsdp', 'expert')), may hold values from -6 to 6
- residual: bfloat16 [16384, 7168], P(('fsdp', 'expert', 'tensor')), may hold values from -6 to 6
- gain: float32 [7168], replicated, may hold values from 0.1 to 1.9
- expert_ids: int32 [16384, 8], P(('fsdp', 'expert', 'tensor')), may hold values from 0 to 255, all different within a row; in each aligned block of 128 rows (0 to 127, 128 to 255, ...) at most 5 rows name the same one
- gate_vals: float32 [16384, 8], P(('fsdp', 'expert', 'tensor')), may hold values from 0.1 to 1
- w_gate: bfloat16 [8, 7168, 2048], P('expert', 'fsdp', 'tensor'), may hold values from -0.0625 to 0.0625
- w_up: bfloat16 [8, 7168, 2048], P('expert', 'fsdp', 'tensor'), may hold values from -0.0625 to 0.0625
- w_down: bfloat16 [8, 2048, 7168], P('expert', 'tensor', 'fsdp'), may hold values from -0.125 to 0.125
Outputs:
- hidden: bfloat16 [16384, 7168], P(('fsdp', 'expert', 'tensor'))
- moe_out: bfloat16 [16384, 7168], P(('fsdp', 'expert', 'tensor'))
The draws below stay inside these ranges and needn't reach their ends.
Inputs may be any that keep to these rules, and one draw needn't show every extreme that they name: `expert_ids`: each row names 8 different experts. Within the rows of one device an expert is named at most 5 times.
All inputs are finite; a program needn't handle non-finite values.
Results may differ from the reference program's by a relative error of at most 0.03.
Values may be sent and summed in bfloat16 or wider, within the bound.
No kernel may reach another device: no remote copies, remote signals or barrier semaphores. Data moves between devices by JAX's collectives and lax.ppermute only.
A program may use at most 128 MiB of HBM per device.

```python
import math
import jax
import jax.numpy as jnp
import numpy as np
from jax import lax

D = 7168
FF = 2048
ROUTED = 256
TOP = 8
TOK_DEV = 128
TOKENS = 16384
CAP = 5
WINDOW = 8
N_EXPERT = 8
N_TENSOR = 4


def block_levels(own_key, shape, pieces, low, high):
    level = 1.0
    for position, blocks in pieces:
        steps = jax.random.uniform(jax.random.fold_in(jax.random.fold_in(own_key, 6), position), (blocks,), jnp.float32, low / len(pieces), high / len(pieces))
        level = level * jnp.repeat(jnp.exp(steps), shape[position] // blocks).reshape((-1,) + (1,) * (len(shape) - 1 - position))
    return level


def deal_out(key, own, number, rows, number_of, top, reach, skew):
    order = jax.random.permutation(key, number_of)
    crowded, usual = load_shares(number_of, rows * top, reach, skew, True), load_shares(number_of, rows * top, reach, skew, False)
    places = jnp.arange(number_of)

    def named(lengths, turn):
        used = int((lengths > 0).sum())
        fixed = max(1, used // 4)
        shifted = fixed + (places - fixed + turn * (used - fixed)) % max(1, number_of - fixed)
        return jnp.zeros((number_of,), jnp.int32).at[order[jnp.where(places < fixed, places, shifted)]].set(jnp.asarray(lengths, jnp.int32))

    lengths = jnp.where(number % 4 == 0, named(crowded, number // 4), named(usual, number - number // 4 - 1))
    mixed = jax.random.permutation(jax.random.fold_in(own, 3), number_of)
    giver, taker = mixed[0:number_of // 2 * 2:2], mixed[1:number_of // 2 * 2:2]
    slack = jnp.minimum(lengths[giver] - 1, reach - lengths[taker]) // 2
    slack = jnp.where((giver == order[0]) | (taker == order[0]) | (lengths[taker] == 0), 0, jnp.maximum(slack, 0))
    shifted = jax.random.randint(jax.random.fold_in(own, 4), (number_of // 2,), 0, 1 << 20) % (slack + 1)
    lengths = lengths.at[giver].add(-shifted).at[taker].add(shifted)
    items = jnp.searchsorted(jnp.cumsum(lengths), jnp.arange(rows * top), side="right").astype(jnp.int32)
    grid = items.reshape(top, rows).T
    grid = grid[jax.random.permutation(jax.random.fold_in(own, 1), rows)]
    turn = jax.random.randint(jax.random.fold_in(own, 2), (rows, 1), 0, top)
    return jnp.take_along_axis(grid, (jnp.arange(top)[None, :] + turn) % top, axis=1)


def load_shares(amount, total, bound, slope, full):
    weights = [(1 << 20) // math.isqrt(rank ** slope) + 1 for rank in range(1, amount + 1)]
    largest = bound if full else min(bound, max(-(-total // amount), total * weights[0] // sum(weights)))
    least = 1 if total - largest >= amount - 1 else 0
    given, rest = [largest] + [least] * (amount - 1), total - largest - least * (amount - 1)
    while rest > 0:
        free = [i for i in range(1, amount) if given[i] < largest] or [i for i in range(1, amount) if given[i] < bound]
        pool, budget = sum([weights[i] for i in free]), rest
        for i in free:
            extra = min(bound - given[i], max(1, budget * weights[i] // pool), rest)
            given[i] = given[i] + extra
            rest = rest - extra
    return np.array(given)


def scatter_about(key, extent, scale, most, shards=(), held_as=jnp.bfloat16):
    array = jax.random.normal(key, extent, jnp.float32) * scale
    if len(shards) > 0:
        array = block_levels(key, extent, shards, -0.22, 0.18) * array
    return jnp.clip(array, min=-most, max=most).astype(held_as)


def setup_inputs(seed: int = 0) -> dict:
    splits = jax.random.split(jax.random.key(seed), 9)
    attn_partial = scatter_about(splits[0], (N_TENSOR, TOKENS, D), 0.7, 6.0, ((0, 4), (1, 32)))
    residual = scatter_about(splits[1], (TOKENS, D), 1.0, 6.0, ((0, 128),))
    gain = jnp.clip(1.0 + 0.18 * jax.random.normal(splits[2], (D,), jnp.float32), 0.1, 1.9)
    expert_ids_keys = jax.random.split(jax.random.fold_in(splits[3], 1), TOKENS // TOK_DEV)
    expert_ids_turns = jax.random.permutation(jax.random.fold_in(splits[3], 3), TOKENS // TOK_DEV)
    expert_ids = jax.vmap(lambda own, number: deal_out(jax.random.fold_in(splits[3], 2), own, number, TOK_DEV, ROUTED, TOP, CAP, 1))(expert_ids_keys, expert_ids_turns).reshape((TOKENS, TOP))
    gate_vals = jnp.clip(jnp.exp(math.log(1.0) - 2.3025851 * jax.random.uniform(splits[4], (TOKENS, TOP), jnp.float32) ** block_levels(splits[4], (TOKENS, TOP), ((0, 128),), -0.2, 0.2)), 0.1, 1.0)
    w_gate = scatter_about(splits[5], (WINDOW, D, FF), D ** -0.5, 0.0625, ((0, 8), (1, 4), (2, 4)))
    w_up = scatter_about(splits[6], (WINDOW, D, FF), D ** -0.5, 0.0625, ((0, 8), (1, 4), (2, 4)))
    w_down = scatter_about(splits[7], (WINDOW, FF, D), FF ** -0.5, 0.125, ((0, 8), (1, 4), (2, 4)))
    return dict(attn_partial=attn_partial, residual=residual, gain=gain, expert_ids=expert_ids, gate_vals=gate_vals, w_gate=w_gate, w_up=w_up, w_down=w_down)


quant_range = 240.0

def quantize(hidden, gain):
    values = hidden.astype(jnp.float32)
    meansq = lax.optimization_barrier(jnp.mean(values * values, axis=-1, keepdims=True))
    normed = values * lax.rsqrt(meansq + 1e-06) * gain
    blocks = normed.reshape(normed.shape[0], -1, 128)
    largest = lax.optimization_barrier(jnp.max(jnp.abs(blocks), axis=-1))
    scales = ((largest + 1e-06) / quant_range).astype(jnp.bfloat16)
    quantized = (blocks / scales.astype(jnp.float32)[..., None]).astype(jnp.bfloat16)
    return (quantized.reshape(normed.shape), scales)

def reference(attn_partial, residual, gain, expert_ids, gate_vals, w_gate, w_up, w_down):
    head_total = attn_partial[0].astype(jnp.float32)
    for group in range(1, N_TENSOR):
        head_total = head_total + attn_partial[group].astype(jnp.float32)
    hidden = (residual.astype(jnp.float32) + head_total).astype(jnp.bfloat16)
    quantized, scales = quantize(hidden, gain)
    nblock = TOKENS // TOK_DEV
    nscale = D // 128
    qblocks = quantized.reshape(nblock, TOK_DEV, D)
    sblocks = scales.reshape(nblock, TOK_DEV, nscale)
    id_blocks = expert_ids.reshape(nblock, TOK_DEV, TOP)
    gate_blocks = gate_vals.reshape(nblock, TOK_DEV, TOP)
    block_index = jnp.broadcast_to(jnp.arange(nblock, dtype=jnp.int32)[:, None], (nblock, TOK_DEV))
    local_rows = jnp.broadcast_to(jnp.arange(TOK_DEV, dtype=jnp.int32)[None, :], (nblock, TOK_DEV))
    column_block = jnp.arange(nblock, dtype=jnp.int32)[:, None]
    width_part = FF // N_TENSOR
    mixture = jnp.zeros((nblock, TOK_DEV, D), jnp.float32)
    for expert in range(N_EXPERT):
        matched = id_blocks == expert
        routed = jnp.any(matched, axis=-1)
        weight = lax.optimization_barrier(jnp.sum(jnp.where(matched, gate_blocks, jnp.float32(0.0)), axis=-1))
        slots = (jnp.cumsum(routed.astype(jnp.int32), axis=1) - 1).astype(jnp.int32)
        target = jnp.where(routed, slots, CAP).astype(jnp.int32)
        source_rows = jnp.zeros((nblock, CAP), jnp.int32).at[block_index, target].set(local_rows, mode='drop')
        filled = jnp.zeros((nblock, CAP), jnp.float32).at[block_index, target].set(1.0, mode='drop')
        picked = qblocks[column_block, source_rows].astype(jnp.float32) * filled[..., None]
        picked_scales = sblocks[column_block, source_rows].astype(jnp.float32) * filled[..., None]
        inputs = picked.reshape(nblock * CAP, nscale, 128) * picked_scales.reshape(nblock * CAP, nscale)[..., None]
        inputs = inputs.reshape(nblock * CAP, D).astype(jnp.bfloat16)
        gate_part = jnp.dot(inputs, w_gate[expert], preferred_element_type=jnp.float32)
        up_part = jnp.dot(inputs, w_up[expert], preferred_element_type=jnp.float32)
        middle = (jax.nn.silu(gate_part) * up_part).astype(jnp.bfloat16)
        outputs = jnp.zeros((nblock * CAP, D), jnp.float32)
        for group in range(N_TENSOR):
            lower = group * width_part
            share = jnp.dot(middle[:, lower:lower + width_part], w_down[expert][lower:lower + width_part], preferred_element_type=jnp.float32)
            outputs = outputs + share.astype(jnp.bfloat16).astype(jnp.float32)
        outputs = outputs.reshape(nblock, CAP, D)
        taken = outputs[column_block, jnp.clip(slots, 0, CAP - 1).astype(jnp.int32)]
        mixture = mixture + (weight * routed.astype(jnp.float32))[..., None] * taken
    moe_out = mixture.reshape(TOKENS, D).astype(jnp.bfloat16)
    return (hidden, moe_out)
```

```python
import jax
import jax.numpy as jnp
from jax import lax
from jax.sharding import Mesh, PartitionSpec as P

CAP = 5
FRONT = 40
RING = 4
SWAP = [(0, 1), (1, 0)]


def shift(value, steps):
    return lax.ppermute(value, "x", [(j, (j + steps) % RING) for j in range(RING)])


def pick(onehot, rows):
    return jnp.dot(onehot, rows, preferred_element_type=jnp.float32)


def local(attn_partial, residual, gain, expert_ids, gate_vals, w_gate, w_up, w_down):
    count, width = residual.shape
    half = width // 2
    quarter = width // 4
    f32, bf = jnp.float32, jnp.bfloat16
    x = lax.axis_index("x")
    core = lax.axis_index("core")
    zh = lax.axis_index("zh")
    attn = attn_partial[0].reshape(RING, count, width)
    wg, wu, wd = w_gate[0], w_up[0], w_down[0]
    wg2 = lax.ppermute(wg, "core", SWAP)
    wu2 = lax.ppermute(wu, "core", SWAP)
    wd2 = lax.ppermute(wd, "core", SWAP)

    with jax.named_scope("routing"):
        experts = jnp.arange(8, dtype=jnp.int32)
        matched = expert_ids[:, :, None] == experts[None, None, :]
        routed = jnp.any(matched, axis=1)
        weight = jnp.sum(jnp.where(matched, gate_vals[:, :, None], 0.0), axis=1)
        anyone = jnp.any(routed, axis=1)
        flags = jnp.concatenate([routed, anyone[:, None]], axis=1).astype(bf)
        token = jnp.arange(count, dtype=jnp.int32)
        tri = (token[:, None] >= token[None, :]).astype(bf)
        upto = pick(tri, flags).astype(jnp.int32)
        slots = upto[:, :8] - 1
        ahead = upto[:, 8]
        pos = jnp.where(anyone, ahead - 1, ahead[-1] + token - ahead)
        poses = [pos] + [shift(pos, -k) for k in (1, 2, 3)]
        places = [
            (p[None, :] == jnp.arange(count, dtype=jnp.int32)[:, None]).astype(bf) for p in poses
        ]
        placing = (
            (slots.T[:, None, :] == jnp.arange(CAP, dtype=jnp.int32)[None, :, None])
            & routed.T[:, None, :]
        ).reshape(8 * CAP, count)

    def head_sum(rows, source, keep):
        sent = [
            pick(places[k][rows], lax.dynamic_index_in_dim(source, (x + k) % RING, 0, False)).astype(bf)
            for k in (1, 2, 3)
        ]
        got = [shift(sent[k - 1], k) for k in (1, 2, 3)]
        own = pick(places[0][rows], lax.dynamic_index_in_dim(source, x, 0, False))
        total = own + got[0].astype(f32) + got[1].astype(f32) + got[2].astype(f32)
        return (pick(places[0][rows], keep) + total).astype(bf)

    front, back = slice(0, FRONT), slice(FRONT, count)
    with jax.named_scope("front_sum"):
        hidden_front = head_sum(front, attn, residual)
    with jax.named_scope("norm_dispatch"):
        values = hidden_front.astype(f32)
        meansq = jnp.mean(values * values, axis=-1, keepdims=True)
        normed = (values * lax.rsqrt(meansq + 1e-06) * gain).astype(bf)
        select = pick(placing.astype(bf), places[0][front].T).astype(bf)
        rows = pick(select, normed).astype(bf)
        rows = rows.reshape(4, 2, CAP, 2, 2, quarter)
        rows = jnp.where(core == 0, rows, rows[:, :, :, :, ::-1])
        rows = rows.transpose(3, 0, 1, 2, 4, 5).reshape(16, CAP, half)
    grid = ("zh", "y", "zl")
    with jax.named_scope("rows_out"):
        got = lax.all_to_all(rows, grid, split_axis=0, concat_axis=0, tiled=True)
        got = got.reshape(16 * CAP, half)
        inputs = jnp.concatenate([got] + [shift(got, k) for k in (1, 2, 3)], axis=0)
    with jax.named_scope("gate_up"):
        first, second = inputs[:, :quarter], inputs[:, quarter:]
        both = jnp.concatenate(
            [pick(first, wg) + pick(second, wg2), pick(first, wu) + pick(second, wu2)], axis=1
        )
        both = both.reshape(2, 8 * 16 * CAP // 4, -1)
        away = lax.ppermute(
            lax.dynamic_index_in_dim(both, 1 - zh, 0, False).astype(bf), "zh", SWAP
        )
        mine = lax.dynamic_index_in_dim(both, zh, 0, False) + away.astype(f32)
        ff = wg.shape[1]
        middle = (jax.nn.silu(mine[:, :ff]) * mine[:, ff:]).astype(bf)
    with jax.named_scope("down"):
        other = lax.ppermute(middle, "zh", SWAP)
        middle = jnp.where(
            zh == 0,
            jnp.concatenate([middle, other], axis=0),
            jnp.concatenate([other, middle], axis=0),
        )
        out = jnp.concatenate([pick(middle, wd), pick(middle, wd2)], axis=1).reshape(RING, 16 * CAP, half)
        total = out[0].astype(bf).astype(f32)
        for k in (1, 2, 3):
            total = total + shift(out[k].astype(bf), -k).astype(f32)
    with jax.named_scope("rows_back"):
        back_rows = lax.all_to_all(
            total.astype(bf).reshape(16, CAP, half), grid, split_axis=0, concat_axis=0, tiled=True
        )
        back_rows = back_rows.reshape(2, 8, CAP, 2, quarter)
        back_rows = jnp.where(core == 0, back_rows, back_rows[:, :, :, ::-1])
        back_rows = back_rows.transpose(1, 2, 0, 3, 4).reshape(8 * CAP, width)
    with jax.named_scope("mix"):
        factor = (
            placing.reshape(8, CAP, count).astype(f32) * weight.T[:, None, :]
        ).reshape(8 * CAP, count).T
        high = factor.astype(bf)
        low = (factor - high.astype(f32)).astype(bf)
        moe_out = (pick(high, back_rows) + pick(low, back_rows)).astype(bf)

    with jax.named_scope("back_sum"):
        late, late_residual, _ = lax.optimization_barrier((attn, residual, rows))
        hidden_back = head_sum(back, late, late_residual)
        hidden = pick(places[0].T, jnp.concatenate([hidden_front, hidden_back], axis=0)).astype(bf)
    return hidden, moe_out


def solution(mesh):
    grid = Mesh(mesh.devices.reshape(2, 2, 4, 2, 4), ("zh", "core", "y", "zl", "x"))
    group = ("zh", "core", "y", "zl")
    token = P(group + ("x",), None)
    placed = (
        P("x", group, None),
        token,
        P(),
        token,
        token,
        P(("y", "zl"), ("zh", "core"), "x"),
        P(("y", "zl"), ("zh", "core"), "x"),
        P(("y", "zl"), "x", ("zh", "core")),
    )
    return jax.shard_map(
        local, mesh=grid, in_specs=placed, out_specs=(token, token), check_vma=False
    )
```

```python
import jax
import jax.numpy as jnp
from jax import lax
from jax.experimental import pallas as pl
from jax.experimental.pallas import tpu as pltpu
from jax.sharding import Mesh, PartitionSpec as P

CAP = 5
EXPERTS = 8
FRONT = EXPERTS * CAP
RING = 4
SWAP = [(0, 1), (1, 0)]
TILE = 896
SEAT = 8
PIECES = (2, 3, 3)
F32, BF = jnp.float32, jnp.bfloat16
VMEM_LIMIT = 14 * 1024 * 1024
VMEM_ALL = 57 * 1024 * 1024


def shift(value, steps):
    return lax.ppermute(value, "x", [(j, (j + steps) % RING) for j in range(RING)])


def ring_sum(far, up, down, beside=None):
    far_first, far_last = shift(far[0], 1), shift(far[1], -1)
    up_last, down_first = shift(up[1], 1), shift(down[0], -1)
    if beside is not None:
        far_first, far_last, beside = lax.optimization_barrier((far_first, far_last, beside))
    up_first = shift((up[0].astype(F32) + far_first.astype(F32)).astype(BF), 1)
    down_last = shift((down[1].astype(F32) + far_last.astype(F32)).astype(BF), -1)
    return (up_first, up_last), (down_first, down_last), beside


def ring_gather(first, last):
    first_up, last_down = shift(first, 1), shift(last, -1)
    last_up, first_down = shift(last, 1), shift(first, -1)
    first_far, last_far = shift(first_up, 1), shift(last_down, -1)
    return [(first, last), (first_up, last_up), (first_far, last_far), (first_down, last_down)]


def dot(a, b):
    return jnp.dot(a, b, preferred_element_type=F32)


def params(limit=VMEM_LIMIT):
    return pltpu.CompilerParams(vmem_limit_bytes=limit)


def cost(flops, size):
    return pl.CostEstimate(flops=int(flops), bytes_accessed=int(size), transcendentals=0)


def onehot(first, rows, pos):
    index = lax.broadcasted_iota(jnp.int32, (rows, pos.shape[1]), 0) + first
    return (index == pos).astype(BF)


def fetch(source, target, sem):
    copy = pltpu.make_async_copy(source, target, sem)
    copy.start()
    return copy


def select_rows(where, attn, poses, rows, distances):
    count = poses.shape[1]
    width = attn.shape[1]
    number = len(distances)
    half = width // 2

    def kernel(where_ref, attn_ref, poses, *refs):
        held, sems = refs[-2:]
        copies = []
        for n, k in enumerate(distances):
            block = pl.multiple_of(lax.rem(where_ref[0] + k, RING) * count, count)
            for c in range(2):
                at = pl.ds(c * half, half)
                copies.append(
                    fetch(attn_ref.at[pl.ds(block, count), at], held.at[n, :, at], sems.at[n, c])
                )
        for n, k in enumerate(distances):
            pick = onehot(0, rows, poses[k : k + 1, :])
            for c in range(2):
                copies[2 * n + c].wait()
                at = slice(c * half, (c + 1) * half)
                refs[2 * n + c][...] = dot(pick, held[n, :, at]).astype(BF)

    vmem = pl.BlockSpec(memory_space=pltpu.VMEM)
    return pl.pallas_call(
        kernel,
        in_specs=[pl.BlockSpec(memory_space=pltpu.SMEM), pl.BlockSpec(memory_space=pl.ANY), vmem],
        out_specs=[vmem] * (2 * number),
        out_shape=[jax.ShapeDtypeStruct((rows, half), BF)] * (2 * number),
        scratch_shapes=[
            pltpu.VMEM((number, count, width), BF),
            pltpu.SemaphoreType.DMA((number, 2)),
        ],
        compiler_params=params(VMEM_ALL),
        cost_estimate=cost(2 * number * rows * count * width, 4 * number * count * width),
        name="select_rows",
    )(where, attn, poses)


def own_rows(where, attn, residual, pos, rows):
    count = pos.shape[1]
    width = attn.shape[1]
    quarter = width // 4

    def kernel(where_ref, attn_ref, residual_ref, pos, out, held, sems):
        block = pl.multiple_of(where_ref[0] * count, count)
        copies = []
        for c in range(4):
            at = pl.ds(c * quarter, quarter)
            copies.append(fetch(attn_ref.at[pl.ds(block, count), at], held.at[0, :, at], sems.at[0, c]))
            copies.append(fetch(residual_ref.at[:, at], held.at[1, :, at], sems.at[1, c]))
        pick = onehot(0, rows, pos[:1, :])
        for c in range(4):
            at = slice(c * quarter, (c + 1) * quarter)
            copies[2 * c].wait()
            copies[2 * c + 1].wait()
            out[:, at] = dot(pick, held[0, :, at]) + dot(pick, held[1, :, at])

    vmem = pl.BlockSpec(memory_space=pltpu.VMEM)
    hbm = pl.BlockSpec(memory_space=pl.ANY)
    return pl.pallas_call(
        kernel,
        in_specs=[pl.BlockSpec(memory_space=pltpu.SMEM), hbm, hbm, vmem],
        out_specs=vmem,
        out_shape=jax.ShapeDtypeStruct((rows, width), F32),
        scratch_shapes=[pltpu.VMEM((2, count, width), BF), pltpu.SemaphoreType.DMA((2, 4))],
        compiler_params=params(VMEM_ALL),
        cost_estimate=cost(4 * rows * count * width, 4 * count * width + 4 * rows * width),
        name="own_rows",
    )(where, attn, residual, pos)


def back_rows(where, attn, poses, first, left, width):
    count = poses.shape[1]
    rows = count - first

    def kernel(where_ref, attn_ref, poses, out, held, sems):
        blocks, copies = [], []
        for k in range(RING):
            blocks.append(lax.rem(where_ref[0] + k, RING))
            at = pl.multiple_of(blocks[k] * count, count)
            copies.append(
                fetch(attn_ref.at[pl.ds(at, count), pl.ds(left, width)], held.at[k], sems.at[k])
            )
        for k in range(RING):
            copies[k].wait()
            out[blocks[k]] = dot(onehot(first, rows, poses[k : k + 1, :]), held[k]).astype(BF)

    vmem = pl.BlockSpec(memory_space=pltpu.VMEM)
    return pl.pallas_call(
        kernel,
        in_specs=[pl.BlockSpec(memory_space=pltpu.SMEM), pl.BlockSpec(memory_space=pl.ANY), vmem],
        out_specs=vmem,
        out_shape=jax.ShapeDtypeStruct((RING, rows, width), BF),
        scratch_shapes=[pltpu.VMEM((RING, count, width), BF), pltpu.SemaphoreType.DMA((RING,))],
        compiler_params=params(VMEM_ALL),
        cost_estimate=cost(8 * rows * count * width, 8 * count * width + 8 * rows * width),
        name="back_rows",
    )(where, attn, poses)


def finish_hidden(where, front, residual, summed, pos, left, earlier=None):
    count, width = residual.shape
    first = front.shape[0]
    rest, wide = summed.shape
    skip = left // TILE

    def kernel(front, residual, summed, pos, *refs):
        back = onehot(first, rest, pos[:1, :])
        tail = (dot(back, residual[...]) + summed[...].astype(F32)).astype(BF)
        total = None
        for place, rows in ((onehot(0, first, pos[:1, :]), front[...]), (back, tail)):
            got = lax.dot_general(place, rows, (((0,), (0,)), ((), ())), preferred_element_type=F32)
            total = got if total is None else total + got
        refs[-1][...] = total.astype(BF)

    in_specs = [
        pl.BlockSpec((first, TILE), lambda i: (0, i + skip)),
        pl.BlockSpec((count, TILE), lambda i: (0, i + skip)),
        pl.BlockSpec((rest, TILE), lambda i: (0, i)),
        pl.BlockSpec((RING, count), lambda i: (0, 0)),
    ]
    operands = [front, residual, summed, pos]
    aliases = {}
    if earlier is not None:
        in_specs.append(pl.BlockSpec(memory_space=pl.ANY))
        operands.append(earlier)
        aliases = {4: 0}
    return pl.pallas_call(
        kernel,
        grid=(wide // TILE,),
        in_specs=in_specs,
        out_specs=pl.BlockSpec((count, TILE), lambda i: (0, i + skip)),
        out_shape=jax.ShapeDtypeStruct((count, width), BF),
        input_output_aliases=aliases,
        compiler_params=params(),
        cost_estimate=cost(4 * count * count * wide, 8 * count * wide),
        name="finish_hidden",
    )(*operands)


def dispatch(where, base, recv, gain, pos, placing):
    rows, width = base.shape
    quarter = width // 4
    seats = placing.shape[0]

    half = width // 2

    def kernel(where_ref, base, r0, r1, r2, r3, gain, pos, placing, front, out, held, came, sems):
        copies = [fetch(r, came.at[n], sems.at[n]) for n, r in enumerate((r0, r1, r2, r3))]
        pick = onehot(0, rows, pos[:1, :])
        square = jnp.zeros((rows, 1), F32)
        for n in range(2):
            copies[n].wait()
            copies[n + 2].wait()
            at = slice(n * half, (n + 1) * half)
            total = base[:, at] + came[n].astype(F32) + came[n + 2].astype(F32)
            rounded = total.astype(BF)
            front[:, at] = rounded
            total = rounded.astype(F32)
            square = square + jnp.sum(total * total, axis=1, keepdims=True)
        scale = lax.rsqrt(square * (1.0 / width) + 1e-06)
        held[...] = (front[...].astype(F32) * scale * gain[...]).astype(BF)
        seat = lax.dot_general(
            placing[...], pick, (((1,), (1,)), ((), ())), preferred_element_type=F32
        ).astype(BF)
        for side in range(2):
            for n in range(2):
                at = pl.multiple_of((side * 2 + lax.rem(where_ref[1] + n, 2)) * quarter, 128)
                got = dot(seat, held[:, pl.ds(at, quarter)])
                out[side * seats : (side + 1) * seats, n * quarter : (n + 1) * quarter] = got.astype(BF)

    vmem = pl.BlockSpec(memory_space=pltpu.VMEM)
    return pl.pallas_call(
        kernel,
        in_specs=[pl.BlockSpec(memory_space=pltpu.SMEM), vmem]
        + [pl.BlockSpec(memory_space=pl.ANY)] * 4
        + [vmem] * 3,
        out_specs=[vmem] * 2,
        out_shape=[
            jax.ShapeDtypeStruct((rows, width), BF),
            jax.ShapeDtypeStruct((2 * seats, width // 2), BF),
        ],
        scratch_shapes=[
            pltpu.VMEM((rows, width), BF),
            pltpu.VMEM((4, rows, half), BF),
            pltpu.SemaphoreType.DMA((4,)),
        ],
        compiler_params=params(),
        cost_estimate=cost(2 * seats * rows * width, 20 * rows * width),
        name="dispatch",
    )(where, base, *recv, gain, pos, placing)


def gate_up(where, blocks, wg, wg2, wu, wu2):
    per = blocks[0][0].shape[0]
    depth, ff = wg.shape
    keep = 2 * per

    def kernel(where_ref, a0, a1, a2, a3, b0, b1, b2, b3, wg, wg2, wu, wu2, mine, away):
        first = jnp.concatenate([a0[...], a1[...], a2[...], a3[...]], axis=0)
        last = jnp.concatenate([b0[...], b1[...], b2[...], b3[...]], axis=0)
        for n, (w, w2) in enumerate(((wg, wg2), (wu, wu2))):
            total = dot(first, w[...]) + dot(last, w2[...])
            columns = slice(n * ff, (n + 1) * ff)
            low = where_ref[3] == 0
            mine[:, columns] = jnp.where(low, total[:keep], total[keep:])
            away[:, columns] = jnp.where(low, total[keep:], total[:keep]).astype(BF)

    vmem = pl.BlockSpec(memory_space=pltpu.VMEM)
    return pl.pallas_call(
        kernel,
        in_specs=[pl.BlockSpec(memory_space=pltpu.SMEM)] + [vmem] * 12,
        out_specs=[vmem, vmem],
        out_shape=[
            jax.ShapeDtypeStruct((keep, 2 * ff), F32),
            jax.ShapeDtypeStruct((keep, 2 * ff), BF),
        ],
        compiler_params=params(),
        cost_estimate=cost(16 * per * 2 * depth * ff, 8 * per * 2 * depth + 8 * depth * ff),
        name="gate_up",
    )(where, *[a for a, _ in blocks], *[b for _, b in blocks], wg, wg2, wu, wu2)


def down(where, mine, other, wd, wd2):
    rows, ff = mine.shape
    quarter = wd.shape[1]
    per = rows // 2

    def kernel(where_ref, mine, other, wd, wd2, *outs):
        low = where_ref[3] == 0
        first = jnp.where(low, mine[...], other[...])
        second = jnp.where(low, other[...], mine[...])
        both = jnp.concatenate([first, second], axis=0)
        for n, w in enumerate((wd, wd2)):
            for c in range(2):
                got = dot(both, w[:, c * TILE : (c + 1) * TILE]).astype(BF)
                for k in range(RING):
                    outs[2 * k + n][:, c * TILE : (c + 1) * TILE] = got[k * per : (k + 1) * per]

    vmem = pl.BlockSpec(memory_space=pltpu.VMEM)
    return pl.pallas_call(
        kernel,
        in_specs=[pl.BlockSpec(memory_space=pltpu.SMEM), vmem, vmem, vmem, vmem],
        out_specs=[vmem] * 8,
        out_shape=[jax.ShapeDtypeStruct((per, quarter), BF)] * 8,
        compiler_params=params(),
        cost_estimate=cost(8 * rows * ff * quarter, 4 * ff * quarter + 8 * rows * quarter),
        name="down",
    )(where, mine, other, wd, wd2)


def mix(where, returned, high, low):
    rows, half = returned.shape
    seats, count = high.shape
    quarter = half // 2

    def kernel(where_ref, returned, high, low, out):
        for side in range(2):
            for n in range(2):
                part = returned[side * seats : (side + 1) * seats, n * quarter : (n + 1) * quarter]
                total = None
                for factor in (high, low):
                    got = lax.dot_general(
                        factor[...], part, (((0,), (0,)), ((), ())), preferred_element_type=F32
                    )
                    total = got if total is None else total + got
                at = pl.multiple_of((2 * side + lax.rem(where_ref[1] + n, 2)) * quarter, 128)
                out[:, pl.ds(at, quarter)] = total.astype(BF)

    vmem = pl.BlockSpec(memory_space=pltpu.VMEM)
    return pl.pallas_call(
        kernel,
        in_specs=[pl.BlockSpec(memory_space=pltpu.SMEM)] + [vmem] * 3,
        out_specs=vmem,
        out_shape=jax.ShapeDtypeStruct((count, 2 * half), BF),
        compiler_params=params(),
        cost_estimate=cost(8 * seats * half * count, 2 * rows * half + 4 * count * half),
        name="mix",
    )(where, returned, high, low)


def find_seats(ids, gates):
    top, count = ids.shape
    seats = EXPERTS * SEAT

    def kernel(ids, gates, placing, high, low):
        row = lax.broadcasted_iota(jnp.int32, (count, count), 0)
        column = lax.broadcasted_iota(jnp.int32, (count, count), 1)
        tri = (row <= column).astype(BF)
        seat = lax.broadcasted_iota(jnp.int32, (SEAT, count), 0)
        for expert in range(EXPERTS):
            match = ids[...] == expert
            here = jnp.sum(match.astype(F32), axis=0, keepdims=True)
            gate = jnp.sum(jnp.where(match, gates[...], 0.0), axis=0, keepdims=True)
            upto = dot(jnp.broadcast_to(here, (SEAT, count)).astype(BF), tri)
            found = (here > 0.0) & (upto == (seat + 1).astype(F32)) & (seat < CAP)
            picked = found.astype(F32)
            factor = picked * gate
            first = factor.astype(BF)
            at = slice(expert * SEAT, (expert + 1) * SEAT)
            placing[at] = picked
            high[at] = first.astype(F32)
            low[at] = factor - first.astype(F32)

    vmem = pl.BlockSpec(memory_space=pltpu.VMEM)
    out = pl.pallas_call(
        kernel,
        in_specs=[vmem, vmem],
        out_specs=[vmem] * 3,
        out_shape=[jax.ShapeDtypeStruct((seats, count), F32)] * 3,
        compiler_params=params(),
        cost_estimate=cost(2 * seats * count * count, 32 * seats * count),
        name="find_seats",
    )(ids, gates)
    return [a.astype(BF) for a in out]


def reseat(rows, columns):
    row = lax.broadcasted_iota(jnp.int32, (rows, columns), 0)
    column = lax.broadcasted_iota(jnp.int32, (rows, columns), 1)
    if rows < columns:
        return ((row // CAP == column // SEAT) & (row % CAP == column % SEAT)).astype(BF)
    return ((row // SEAT == column // CAP) & (row % SEAT == column % CAP)).astype(BF)


def pack(rows):
    wide, half = rows.shape
    short = wide // SEAT * CAP
    quarter = half // 2

    def kernel(rows, first, last):
        take = reseat(short, wide)
        first[...] = dot(take, rows[:, :quarter]).astype(BF)
        last[...] = dot(take, rows[:, quarter:]).astype(BF)

    vmem = pl.BlockSpec(memory_space=pltpu.VMEM)
    return pl.pallas_call(
        kernel,
        in_specs=[vmem],
        out_specs=[vmem, vmem],
        out_shape=[jax.ShapeDtypeStruct((short, quarter), BF)] * 2,
        compiler_params=params(),
        cost_estimate=cost(2 * short * wide * half, 4 * wide * half),
        name="pack",
    )(rows)


def add_parts(own, behind, ahead):
    short, quarter = own[0].shape
    wide = short // CAP * SEAT

    def kernel(*refs):
        put = reseat(wide, short)
        for n in range(2):
            total = refs[n][...].astype(F32) + refs[2 + n][...].astype(F32) + refs[4 + n][...].astype(F32)
            refs[6][:, n * quarter : (n + 1) * quarter] = dot(put, total.astype(BF)).astype(BF)

    vmem = pl.BlockSpec(memory_space=pltpu.VMEM)
    return pl.pallas_call(
        kernel,
        in_specs=[vmem] * 6,
        out_specs=vmem,
        out_shape=jax.ShapeDtypeStruct((wide, 2 * quarter), BF),
        compiler_params=params(),
        cost_estimate=cost(4 * short * wide * quarter, 20 * short * quarter),
        name="add_parts",
    )(*own, *behind, *ahead)


def local(attn_partial, residual, gain, expert_ids, gate_vals, w_gate, w_up, w_down):
    count, width = residual.shape
    ff = w_gate.shape[2]
    barrier = lax.optimization_barrier
    where = jnp.stack([lax.axis_index(a) for a in ("x", "core", "y", "zh")]).astype(jnp.int32)
    grid = ("zh", "y", "zl")
    attn = attn_partial[0]
    wg, wu, wd = w_gate[0], w_up[0], w_down[0]
    gain = gain.reshape(1, width)

    with jax.named_scope("routing"):
        token = jnp.arange(count, dtype=jnp.int32)
        anyone = jnp.any(expert_ids < EXPERTS, axis=1)
        tri = (token[:, None] >= token[None, :]).astype(BF)
        ahead = dot(tri, anyone[:, None].astype(BF)).astype(jnp.int32)[:, 0]
        pos = jnp.where(anyone, ahead - 1, ahead[-1] + token - ahead).reshape(1, count)
        base = own_rows(where, attn, residual, pos, FRONT)
        poses = jnp.concatenate([pos] + [shift(pos, -k) for k in (1, 2, 3)], axis=0)
        poses, base = barrier((poses, base))

    with jax.named_scope("weight_swap"):
        wg2 = lax.ppermute(wg, "core", SWAP)
        wu2 = lax.ppermute(wu, "core", SWAP)
        wd2 = lax.ppermute(wd, "core", SWAP)

    with jax.named_scope("front_sum"):
        far = select_rows(where, attn, poses, FRONT, (2,))
        far, poses = barrier((far, poses))
        near = select_rows(where, attn, poses, FRONT, (1, 3))
        near, poses, ids, gates = barrier((near, poses, expert_ids.T, gate_vals.T))
        back = [back_rows(where, attn, poses, FRONT, 0, PIECES[0] * TILE)]
        seats = find_seats(ids, gates)
        behind, ahead, (back, seats) = ring_sum(far, near[:2], near[2:], (back, seats))
        placing, high, low = seats
    def head_sum(n, after):
        operand, after = barrier((back[n], after))
        with jax.named_scope("head_sum"):
            summed = lax.psum_scatter(operand, "x", scatter_dimension=0, tiled=True)
        return summed[0], after

    with jax.named_scope("rows_out"):
        front, message = dispatch(where, base, (*behind, *ahead), gain, poses, placing)
        summed0, message = head_sum(0, message)
        late_poses, message = barrier((poses, message))
        left = PIECES[0] * TILE
        for tiles in PIECES[1:]:
            back.append(back_rows(where, attn, late_poses, FRONT, left, tiles * TILE))
            left += tiles * TILE
        whole = lax.all_to_all(message, grid, split_axis=0, concat_axis=0, tiled=True)
        whole, back = barrier((whole, back))
        rows = ring_gather(*pack(whole))
    with jax.named_scope("gate_up"):
        mine, away = gate_up(where, rows, wg, wg2, wu, wu2)
        summed1, away = head_sum(1, away)
        mine = mine + lax.ppermute(away, "zh", SWAP).astype(F32)
        middle = (jax.nn.silu(mine[:, :ff]) * mine[:, ff:]).astype(BF)
        other = lax.ppermute(middle, "zh", SWAP)
    with jax.named_scope("rows_back"):
        outs = down(where, middle, other, wd, wd2)
        total = add_parts(outs[:2], *ring_sum(outs[4:6], outs[6:8], outs[2:4])[:2])
        summed2, total = head_sum(2, total)
        returned = lax.all_to_all(total, grid, split_axis=0, concat_axis=0, tiled=True)
    with jax.named_scope("hidden"):
        hidden, left = None, 0
        for tiles, summed in zip(PIECES, (summed0, summed1, summed2)):
            if left + tiles * TILE == width:
                returned, hidden = barrier((returned, hidden))
            hidden = finish_hidden(where, front, residual, summed, poses, left, hidden)
            left += tiles * TILE
    with jax.named_scope("mix"):
        moe_out = mix(where, returned, high, low)
    return hidden, moe_out


def solution(mesh):
    grid = Mesh(mesh.devices.reshape(2, 2, 4, 2, 4), ("zh", "core", "y", "zl", "x"))
    group = ("zh", "core", "y", "zl")
    token = P(group + ("x",), None)
    placed = (
        P("x", group, None),
        token,
        P(),
        token,
        token,
        P(("y", "zl"), ("zh", "core"), "x"),
        P(("y", "zl"), ("zh", "core"), "x"),
        P(("y", "zl"), "x", ("zh", "core")),
    )
    return jax.shard_map(
        local, mesh=grid, in_specs=placed, out_specs=(token, token), check_vma=False
    )
```

```python
import jax
import jax.numpy as jnp
from jax import lax
from jax.experimental import pallas as pl
from jax.experimental.pallas import tpu as pltpu
from jax.sharding import Mesh, PartitionSpec as P

CAP = 5
EXPERTS = 8
FRONT = EXPERTS * CAP
RING = 4
SWAP = [(0, 1), (1, 0)]
TILE = 896
SEAT = 8
PIECES = (3, 3, 2)
F32, BF = jnp.float32, jnp.bfloat16
VMEM_LIMIT = 14 * 1024 * 1024


def shift(value, steps):
    return lax.ppermute(value, "x", [(j, (j + steps) % RING) for j in range(RING)])


def ring_sum(far, up, down, beside=None):
    far_first, far_last = shift(far[0], 1), shift(far[1], -1)
    up_last, down_first = shift(up[1], 1), shift(down[0], -1)
    if beside is not None:
        far_first, far_last, beside = lax.optimization_barrier((far_first, far_last, beside))
    up_first = shift((up[0].astype(F32) + far_first.astype(F32)).astype(BF), 1)
    down_last = shift((down[1].astype(F32) + far_last.astype(F32)).astype(BF), -1)
    return (up_first, up_last), (down_first, down_last), beside


def ring_gather(first, last):
    first_up, last_down = shift(first, 1), shift(last, -1)
    last_up, first_down = shift(last, 1), shift(first, -1)
    first_far, last_far = shift(first_up, 1), shift(last_down, -1)
    return [(first, last), (first_up, last_up), (first_far, last_far), (first_down, last_down)]


def dot(a, b):
    return jnp.dot(a, b, preferred_element_type=F32)


def params(limit=VMEM_LIMIT):
    return pltpu.CompilerParams(vmem_limit_bytes=limit)


def cost(flops, size):
    return pl.CostEstimate(flops=int(flops), bytes_accessed=int(size), transcendentals=0)


def onehot(first, rows, pos):
    index = lax.broadcasted_iota(jnp.int32, (rows, pos.shape[1]), 0) + first
    return (index == pos).astype(BF)


def block_of(where_ref, distance, count):
    block = lax.rem(where_ref[0] + distance, RING)
    return block, pl.ds(pl.multiple_of(block * count, count), count)


def load(attn, after):
    def kernel(attn, after, out, sem):
        copy = pltpu.make_async_copy(attn, out, sem)
        copy.start()
        copy.wait()

    return pl.pallas_call(
        kernel,
        in_specs=[pl.BlockSpec(memory_space=pl.ANY), pl.BlockSpec(memory_space=pl.ANY)],
        out_specs=pl.BlockSpec(memory_space=pltpu.VMEM),
        out_shape=jax.ShapeDtypeStruct(attn.shape, BF),
        scratch_shapes=[pltpu.SemaphoreType.DMA(())],
        compiler_params=params(),
        cost_estimate=cost(0, 4 * attn.size),
        name="load",
    )(attn, after)


def select_rows(where, attn, poses, rows, distances):
    count = poses.shape[1]
    half = attn.shape[1] // 2
    number = 2 * len(distances)

    def kernel(where_ref, attn, poses, *outs):
        for n, k in enumerate(distances):
            pick = onehot(0, rows, poses[k : k + 1, :])
            _, at = block_of(where_ref, k, count)
            for c in range(2):
                outs[2 * n + c][...] = dot(pick, attn[at, c * half : (c + 1) * half]).astype(BF)

    vmem = pl.BlockSpec(memory_space=pltpu.VMEM)
    return pl.pallas_call(
        kernel,
        in_specs=[pl.BlockSpec(memory_space=pltpu.SMEM), vmem, vmem],
        out_specs=[vmem] * number,
        out_shape=[jax.ShapeDtypeStruct((rows, half), BF)] * number,
        compiler_params=params(),
        cost_estimate=cost(2 * number * rows * count * half, 2 * number * count * half),
        name="select_rows",
    )(where, attn, poses)


def own_rows(where, attn, residual, pos, rows):
    count, width = residual.shape

    def kernel(where_ref, attn, residual, pos, out):
        pick = onehot(0, rows, pos[:1, :])
        _, at = block_of(where_ref, 0, count)
        out[...] = dot(pick, attn[at, :]) + dot(pick, residual[...])

    vmem = pl.BlockSpec(memory_space=pltpu.VMEM)
    return pl.pallas_call(
        kernel,
        in_specs=[pl.BlockSpec(memory_space=pltpu.SMEM), vmem, vmem, vmem],
        out_specs=vmem,
        out_shape=jax.ShapeDtypeStruct((rows, width), F32),
        compiler_params=params(),
        cost_estimate=cost(4 * rows * count * width, 4 * count * width + 4 * rows * width),
        name="own_rows",
    )(where, attn, residual, pos)


def back_rows(where, attn, poses, first, left, widths):
    count = poses.shape[1]
    rows = count - first

    def kernel(where_ref, attn, poses, *outs):
        for k in range(RING):
            block, at = block_of(where_ref, k, count)
            pick = onehot(first, rows, poses[k : k + 1, :])
            start = left
            for out, width in zip(outs, widths):
                out[block] = dot(pick, attn[at, start : start + width]).astype(BF)
                start += width

    vmem = pl.BlockSpec(memory_space=pltpu.VMEM)
    wide = sum(widths)
    return pl.pallas_call(
        kernel,
        in_specs=[pl.BlockSpec(memory_space=pltpu.SMEM), vmem, vmem],
        out_specs=[vmem] * len(widths),
        out_shape=[jax.ShapeDtypeStruct((RING, rows, width), BF) for width in widths],
        compiler_params=params(),
        cost_estimate=cost(8 * rows * count * wide, 8 * count * wide + 8 * rows * wide),
        name="back_rows",
    )(where, attn, poses)


def finish_hidden(where, front, residual, summed, pos, left, earlier=None):
    count, width = residual.shape
    first = front.shape[0]
    rest, wide = summed.shape
    skip = left // TILE

    def kernel(front, residual, summed, pos, *refs):
        back = onehot(first, rest, pos[:1, :])
        tail = (dot(back, residual[...]) + summed[...].astype(F32)).astype(BF)
        total = None
        for place, rows in ((onehot(0, first, pos[:1, :]), front[...]), (back, tail)):
            got = lax.dot_general(place, rows, (((0,), (0,)), ((), ())), preferred_element_type=F32)
            total = got if total is None else total + got
        refs[-1][...] = total.astype(BF)

    in_specs = [
        pl.BlockSpec((first, TILE), lambda i: (0, i + skip)),
        pl.BlockSpec((count, TILE), lambda i: (0, i + skip)),
        pl.BlockSpec((rest, TILE), lambda i: (0, i)),
        pl.BlockSpec((RING, count), lambda i: (0, 0)),
    ]
    operands = [front, residual, summed, pos]
    aliases = {}
    if earlier is not None:
        in_specs.append(pl.BlockSpec(memory_space=pl.ANY))
        operands.append(earlier)
        aliases = {4: 0}
    return pl.pallas_call(
        kernel,
        grid=(wide // TILE,),
        in_specs=in_specs,
        out_specs=pl.BlockSpec((count, TILE), lambda i: (0, i + skip)),
        out_shape=jax.ShapeDtypeStruct((count, width), BF),
        input_output_aliases=aliases,
        compiler_params=params(),
        cost_estimate=cost(4 * count * count * wide, 8 * count * wide),
        name="finish_hidden",
    )(*operands)


def dispatch(where, base, recv, gain, pos, placing):
    rows, width = base.shape
    quarter = width // 4
    seats = placing.shape[0]

    half = width // 2

    def kernel(where_ref, base, r0, r1, r2, r3, gain, pos, placing, front, out, held):
        pick = onehot(0, rows, pos[:1, :])
        square = jnp.zeros((rows, 1), F32)
        for n, (a, b) in enumerate(((r0, r2), (r1, r3))):
            at = slice(n * half, (n + 1) * half)
            total = base[:, at] + a[...].astype(F32) + b[...].astype(F32)
            rounded = total.astype(BF)
            front[:, at] = rounded
            total = rounded.astype(F32)
            square = square + jnp.sum(total * total, axis=1, keepdims=True)
        scale = lax.rsqrt(square * (1.0 / width) + 1e-06)
        held[...] = (front[...].astype(F32) * scale * gain[...]).astype(BF)
        seat = lax.dot_general(
            placing[...], pick, (((1,), (1,)), ((), ())), preferred_element_type=F32
        ).astype(BF)
        for side in range(2):
            for n in range(2):
                at = pl.multiple_of((side * 2 + lax.rem(where_ref[1] + n, 2)) * quarter, 128)
                got = dot(seat, held[:, pl.ds(at, quarter)])
                out[side * seats : (side + 1) * seats, n * quarter : (n + 1) * quarter] = got.astype(BF)

    vmem = pl.BlockSpec(memory_space=pltpu.VMEM)
    return pl.pallas_call(
        kernel,
        in_specs=[pl.BlockSpec(memory_space=pltpu.SMEM)] + [vmem] * 8,
        out_specs=[vmem] * 2,
        out_shape=[
            jax.ShapeDtypeStruct((rows, width), BF),
            jax.ShapeDtypeStruct((2 * seats, width // 2), BF),
        ],
        scratch_shapes=[pltpu.VMEM((rows, width), BF)],
        compiler_params=params(),
        cost_estimate=cost(2 * seats * rows * width, 20 * rows * width),
        name="dispatch",
    )(where, base, *recv, gain, pos, placing)


def gate_up(where, blocks, wg, wg2, wu, wu2):
    per = blocks[0][0].shape[0]
    depth, ff = wg.shape
    keep = 2 * per

    def kernel(where_ref, a0, a1, a2, a3, b0, b1, b2, b3, wg, wg2, wu, wu2, mine, away):
        first = jnp.concatenate([a0[...], a1[...], a2[...], a3[...]], axis=0)
        last = jnp.concatenate([b0[...], b1[...], b2[...], b3[...]], axis=0)
        for n, (w, w2) in enumerate(((wg, wg2), (wu, wu2))):
            total = dot(first, w[...]) + dot(last, w2[...])
            columns = slice(n * ff, (n + 1) * ff)
            low = where_ref[3] == 0
            mine[:, columns] = jnp.where(low, total[:keep], total[keep:])
            away[:, columns] = jnp.where(low, total[keep:], total[:keep]).astype(BF)

    vmem = pl.BlockSpec(memory_space=pltpu.VMEM)
    return pl.pallas_call(
        kernel,
        in_specs=[pl.BlockSpec(memory_space=pltpu.SMEM)] + [vmem] * 12,
        out_specs=[vmem, vmem],
        out_shape=[
            jax.ShapeDtypeStruct((keep, 2 * ff), F32),
            jax.ShapeDtypeStruct((keep, 2 * ff), BF),
        ],
        compiler_params=params(),
        cost_estimate=cost(16 * per * 2 * depth * ff, 8 * per * 2 * depth + 8 * depth * ff),
        name="gate_up",
    )(where, *[a for a, _ in blocks], *[b for _, b in blocks], wg, wg2, wu, wu2)


def down(where, mine, other, wd, wd2):
    rows, ff = mine.shape
    quarter = wd.shape[1]
    per = rows // 2

    def kernel(where_ref, mine, other, wd, wd2, *outs):
        low = where_ref[3] == 0
        first = jnp.where(low, mine[...], other[...])
        second = jnp.where(low, other[...], mine[...])
        both = jnp.concatenate([first, second], axis=0)
        for n, w in enumerate((wd, wd2)):
            for c in range(2):
                got = dot(both, w[:, c * TILE : (c + 1) * TILE]).astype(BF)
                for k in range(RING):
                    outs[2 * k + n][:, c * TILE : (c + 1) * TILE] = got[k * per : (k + 1) * per]

    vmem = pl.BlockSpec(memory_space=pltpu.VMEM)
    return pl.pallas_call(
        kernel,
        in_specs=[pl.BlockSpec(memory_space=pltpu.SMEM), vmem, vmem, vmem, vmem],
        out_specs=[vmem] * 8,
        out_shape=[jax.ShapeDtypeStruct((per, quarter), BF)] * 8,
        compiler_params=params(),
        cost_estimate=cost(8 * rows * ff * quarter, 4 * ff * quarter + 8 * rows * quarter),
        name="down",
    )(where, mine, other, wd, wd2)


def mix(where, returned, high, low):
    rows, half = returned.shape
    seats, count = high.shape
    quarter = half // 2

    def kernel(where_ref, returned, high, low, out):
        for side in range(2):
            for n in range(2):
                part = returned[side * seats : (side + 1) * seats, n * quarter : (n + 1) * quarter]
                total = None
                for factor in (high, low):
                    got = lax.dot_general(
                        factor[...], part, (((0,), (0,)), ((), ())), preferred_element_type=F32
                    )
                    total = got if total is None else total + got
                at = pl.multiple_of((2 * side + lax.rem(where_ref[1] + n, 2)) * quarter, 128)
                out[:, pl.ds(at, quarter)] = total.astype(BF)

    vmem = pl.BlockSpec(memory_space=pltpu.VMEM)
    return pl.pallas_call(
        kernel,
        in_specs=[pl.BlockSpec(memory_space=pltpu.SMEM)] + [vmem] * 3,
        out_specs=vmem,
        out_shape=jax.ShapeDtypeStruct((count, 2 * half), BF),
        compiler_params=params(),
        cost_estimate=cost(8 * seats * half * count, 2 * rows * half + 4 * count * half),
        name="mix",
    )(where, returned, high, low)


def find_seats(ids, gates):
    top, count = ids.shape
    seats = EXPERTS * SEAT

    def kernel(ids, gates, placing, high, low):
        row = lax.broadcasted_iota(jnp.int32, (count, count), 0)
        column = lax.broadcasted_iota(jnp.int32, (count, count), 1)
        tri = (row <= column).astype(BF)
        seat = lax.broadcasted_iota(jnp.int32, (SEAT, count), 0)
        for expert in range(EXPERTS):
            match = ids[...] == expert
            here = jnp.sum(match.astype(F32), axis=0, keepdims=True)
            gate = jnp.sum(jnp.where(match, gates[...], 0.0), axis=0, keepdims=True)
            upto = dot(jnp.broadcast_to(here, (SEAT, count)).astype(BF), tri)
            found = (here > 0.0) & (upto == (seat + 1).astype(F32)) & (seat < CAP)
            picked = found.astype(F32)
            factor = picked * gate
            first = factor.astype(BF)
            at = slice(expert * SEAT, (expert + 1) * SEAT)
            placing[at] = picked
            high[at] = first.astype(F32)
            low[at] = factor - first.astype(F32)

    vmem = pl.BlockSpec(memory_space=pltpu.VMEM)
    out = pl.pallas_call(
        kernel,
        in_specs=[vmem, vmem],
        out_specs=[vmem] * 3,
        out_shape=[jax.ShapeDtypeStruct((seats, count), F32)] * 3,
        compiler_params=params(),
        cost_estimate=cost(2 * seats * count * count, 32 * seats * count),
        name="find_seats",
    )(ids, gates)
    return [a.astype(BF) for a in out]


def reseat(rows, columns):
    row = lax.broadcasted_iota(jnp.int32, (rows, columns), 0)
    column = lax.broadcasted_iota(jnp.int32, (rows, columns), 1)
    if rows < columns:
        return ((row // CAP == column // SEAT) & (row % CAP == column % SEAT)).astype(BF)
    return ((row // SEAT == column // CAP) & (row % SEAT == column % CAP)).astype(BF)


def pack(rows):
    wide, half = rows.shape
    short = wide // SEAT * CAP
    quarter = half // 2

    def kernel(rows, first, last):
        take = reseat(short, wide)
        first[...] = dot(take, rows[:, :quarter]).astype(BF)
        last[...] = dot(take, rows[:, quarter:]).astype(BF)

    vmem = pl.BlockSpec(memory_space=pltpu.VMEM)
    return pl.pallas_call(
        kernel,
        in_specs=[vmem],
        out_specs=[vmem, vmem],
        out_shape=[jax.ShapeDtypeStruct((short, quarter), BF)] * 2,
        compiler_params=params(),
        cost_estimate=cost(2 * short * wide * half, 4 * wide * half),
        name="pack",
    )(rows)


def add_parts(own, behind, ahead):
    short, quarter = own[0].shape
    wide = short // CAP * SEAT

    def kernel(*refs):
        put = reseat(wide, short)
        for n in range(2):
            total = refs[n][...].astype(F32) + refs[2 + n][...].astype(F32) + refs[4 + n][...].astype(F32)
            refs[6][:, n * quarter : (n + 1) * quarter] = dot(put, total.astype(BF)).astype(BF)

    vmem = pl.BlockSpec(memory_space=pltpu.VMEM)
    return pl.pallas_call(
        kernel,
        in_specs=[vmem] * 6,
        out_specs=vmem,
        out_shape=jax.ShapeDtypeStruct((wide, 2 * quarter), BF),
        compiler_params=params(),
        cost_estimate=cost(4 * short * wide * quarter, 20 * short * quarter),
        name="add_parts",
    )(*own, *behind, *ahead)


def local(attn_partial, residual, gain, expert_ids, gate_vals, w_gate, w_up, w_down):
    count, width = residual.shape
    ff = w_gate.shape[2]
    barrier = lax.optimization_barrier
    where = jnp.stack([lax.axis_index(a) for a in ("x", "core", "y", "zh")]).astype(jnp.int32)
    grid = ("zh", "y", "zl")
    attn = attn_partial[0]
    wg, wu, wd = w_gate[0], w_up[0], w_down[0]
    gain = gain.reshape(1, width)

    with jax.named_scope("routing"):
        token = jnp.arange(count, dtype=jnp.int32)
        anyone = jnp.any(expert_ids < EXPERTS, axis=1)
        tri = (token[:, None] >= token[None, :]).astype(BF)
        ahead = dot(tri, anyone[:, None].astype(BF)).astype(jnp.int32)[:, 0]
        pos = jnp.where(anyone, ahead - 1, ahead[-1] + token - ahead).reshape(1, count)
        attn = load(attn, pos)
        poses = jnp.concatenate([pos] + [shift(pos, -k) for k in (1, 2, 3)], axis=0)

    with jax.named_scope("weight_swap"):
        wg2 = lax.ppermute(wg, "core", SWAP)
        wu2 = lax.ppermute(wu, "core", SWAP)
        wd2 = lax.ppermute(wd, "core", SWAP)

    back, summed = [], {}

    def head_sum(n, after):
        operand, after = barrier((back[n], after))
        with jax.named_scope("head_sum"):
            summed[n] = lax.psum_scatter(operand, "x", scatter_dimension=0, tiled=True)[0]
        return after

    with jax.named_scope("front_sum"):
        attn, poses = barrier((attn, poses))
        far = select_rows(where, attn, poses, FRONT, (2,))
        far, poses = barrier((far, poses))
        near = select_rows(where, attn, poses, FRONT, (1, 3))
        near, poses, ids, gates = barrier((near, poses, expert_ids.T, gate_vals.T))
        pieces = [tiles * TILE for tiles in PIECES]
        back += back_rows(where, attn, poses, FRONT, 0, pieces[:1])
        seats = find_seats(ids, gates)
        base = own_rows(where, attn, residual, poses, FRONT)
        beside = (back[0], seats, wg2, wu2, wd2)
        behind, ahead, (_, seats, wg2, wu2, wd2) = ring_sum(far, near[:2], near[2:], beside)
        placing, high, low = seats
    with jax.named_scope("rows_out"):
        behind, ahead = head_sum(0, (behind, ahead))
        front, message = dispatch(where, base, (*behind, *ahead), gain, poses, placing)
        late_poses, message = barrier((poses, message))
        back += back_rows(where, attn, late_poses, FRONT, pieces[0], pieces[1:])
        whole = lax.all_to_all(message, grid, split_axis=0, concat_axis=0, tiled=True)
        whole, back[1:] = barrier((whole, back[1:]))
        rows = ring_gather(*pack(whole))
    with jax.named_scope("gate_up"):
        rows = head_sum(1, rows)
        mine, away = gate_up(where, rows, wg, wg2, wu, wu2)
        mine = mine + lax.ppermute(away, "zh", SWAP).astype(F32)
        middle = (jax.nn.silu(mine[:, :ff]) * mine[:, ff:]).astype(BF)
        other = lax.ppermute(middle, "zh", SWAP)
    with jax.named_scope("rows_back"):
        outs = down(where, middle, other, wd, wd2)
        came = head_sum(2, ring_sum(outs[4:6], outs[6:8], outs[2:4])[:2])
        total = add_parts(outs[:2], *came)
        returned = lax.all_to_all(total, grid, split_axis=0, concat_axis=0, tiled=True)
    with jax.named_scope("hidden"):
        hidden = finish_hidden(where, front, residual, summed[0], poses, 0)
        hidden = finish_hidden(where, front, residual, summed[1], poses, pieces[0], hidden)
        returned, hidden = barrier((returned, hidden))
    with jax.named_scope("mix"):
        moe_out = mix(where, returned, high, low)
    with jax.named_scope("hidden"):
        moe_out, hidden = barrier((moe_out, hidden))
        hidden = finish_hidden(where, front, residual, summed[2], poses, sum(pieces[:2]), hidden)
    return hidden, moe_out


def solution(mesh):
    grid = Mesh(mesh.devices.reshape(2, 2, 4, 2, 4), ("zh", "core", "y", "zl", "x"))
    group = ("zh", "core", "y", "zl")
    token = P(group + ("x",), None)
    placed = (
        P("x", group, None),
        token,
        P(),
        token,
        token,
        P(("y", "zl"), ("zh", "core"), "x"),
        P(("y", "zl"), ("zh", "core"), "x"),
        P(("y", "zl"), "x", ("zh", "core")),
    )
    return jax.shard_map(
        local, mesh=grid, in_specs=placed, out_specs=(token, token), check_vma=False
    )
```

```python
import jax
import jax.numpy as jnp
from jax import lax
from jax.experimental import pallas as pl
from jax.experimental.pallas import tpu as pltpu
from jax.sharding import Mesh, PartitionSpec as P

CAP = 5
EXPERTS = 8
FRONT = EXPERTS * CAP
RING = 4
SWAP = [(0, 1), (1, 0)]
TILE = 896
SEAT = 8
PIECES = (3, 3, 2)
F32, BF = jnp.float32, jnp.bfloat16
VMEM_LIMIT = 14 * 1024 * 1024


def shift(value, steps):
    return lax.ppermute(value, "x", [(j, (j + steps) % RING) for j in range(RING)])


def ring_sum(far, up, down, beside=None):
    far_first, far_last = shift(far[0], 1), shift(far[1], -1)
    up_last, down_first = shift(up[1], 1), shift(down[0], -1)
    if beside is not None:
        far_first, far_last, beside = lax.optimization_barrier((far_first, far_last, beside))
    up_first = shift((up[0].astype(F32) + far_first.astype(F32)).astype(BF), 1)
    down_last = shift((down[1].astype(F32) + far_last.astype(F32)).astype(BF), -1)
    return (up_first, up_last), (down_first, down_last), beside


def ring_gather(first, last):
    first_up, last_down = shift(first, 1), shift(last, -1)
    last_up, first_down = shift(last, 1), shift(first, -1)
    first_far, last_far = shift(first_up, 1), shift(last_down, -1)
    return [(first, last), (first_up, last_up), (first_far, last_far), (first_down, last_down)]


def dot(a, b):
    return jnp.dot(a, b, preferred_element_type=F32)


def params(limit=VMEM_LIMIT):
    return pltpu.CompilerParams(vmem_limit_bytes=limit)


def cost(flops, size):
    return pl.CostEstimate(flops=int(flops), bytes_accessed=int(size), transcendentals=0)


def onehot(first, rows, pos):
    index = lax.broadcasted_iota(jnp.int32, (rows, pos.shape[1]), 0) + first
    return (index == pos).astype(BF)


def block_of(where_ref, distance, count):
    block = lax.rem(where_ref[0] + distance, RING)
    return block, pl.ds(pl.multiple_of(block * count, count), count)


def load(attn, after):
    def kernel(attn, after, out, sem):
        copy = pltpu.make_async_copy(attn, out, sem)
        copy.start()
        copy.wait()

    return pl.pallas_call(
        kernel,
        in_specs=[pl.BlockSpec(memory_space=pl.ANY), pl.BlockSpec(memory_space=pl.ANY)],
        out_specs=pl.BlockSpec(memory_space=pltpu.VMEM),
        out_shape=jax.ShapeDtypeStruct(attn.shape, BF),
        scratch_shapes=[pltpu.SemaphoreType.DMA(())],
        compiler_params=params(),
        cost_estimate=cost(0, 4 * attn.size),
        name="load",
    )(attn, after)


def select_rows(where, attn, poses, rows, distances):
    count = poses.shape[1]
    half = attn.shape[1] // 2
    number = 2 * len(distances)

    def kernel(where_ref, attn, poses, *outs):
        for n, k in enumerate(distances):
            pick = onehot(0, rows, poses[k : k + 1, :])
            _, at = block_of(where_ref, k, count)
            for c in range(2):
                outs[2 * n + c][...] = dot(pick, attn[at, c * half : (c + 1) * half]).astype(BF)

    vmem = pl.BlockSpec(memory_space=pltpu.VMEM)
    return pl.pallas_call(
        kernel,
        in_specs=[pl.BlockSpec(memory_space=pltpu.SMEM), vmem, vmem],
        out_specs=[vmem] * number,
        out_shape=[jax.ShapeDtypeStruct((rows, half), BF)] * number,
        compiler_params=params(),
        cost_estimate=cost(2 * number * rows * count * half, 2 * number * count * half),
        name="select_rows",
    )(where, attn, poses)


def own_rows(where, attn, residual, pos, rows):
    count, width = residual.shape

    def kernel(where_ref, attn, residual, pos, out):
        pick = onehot(0, rows, pos[:1, :])
        _, at = block_of(where_ref, 0, count)
        out[...] = dot(pick, attn[at, :]) + dot(pick, residual[...])

    vmem = pl.BlockSpec(memory_space=pltpu.VMEM)
    return pl.pallas_call(
        kernel,
        in_specs=[pl.BlockSpec(memory_space=pltpu.SMEM), vmem, vmem, vmem],
        out_specs=vmem,
        out_shape=jax.ShapeDtypeStruct((rows, width), F32),
        compiler_params=params(),
        cost_estimate=cost(4 * rows * count * width, 4 * count * width + 4 * rows * width),
        name="own_rows",
    )(where, attn, residual, pos)


def back_rows(where, attn, poses, first, left, widths):
    count = poses.shape[1]
    rows = count - first

    def kernel(where_ref, attn, poses, *outs):
        for k in range(RING):
            block, at = block_of(where_ref, k, count)
            pick = onehot(first, rows, poses[k : k + 1, :])
            start = left
            for out, width in zip(outs, widths):
                out[block] = dot(pick, attn[at, start : start + width]).astype(BF)
                start += width

    vmem = pl.BlockSpec(memory_space=pltpu.VMEM)
    wide = sum(widths)
    return pl.pallas_call(
        kernel,
        in_specs=[pl.BlockSpec(memory_space=pltpu.SMEM), vmem, vmem],
        out_specs=[vmem] * len(widths),
        out_shape=[jax.ShapeDtypeStruct((RING, rows, width), BF) for width in widths],
        compiler_params=params(),
        cost_estimate=cost(8 * rows * count * wide, 8 * count * wide + 8 * rows * wide),
        name="back_rows",
    )(where, attn, poses)


def finish_hidden(where, front, residual, summed, pos, left, earlier=None):
    count, width = residual.shape
    first = front.shape[0]
    rest, wide = summed.shape
    skip = left // TILE

    def kernel(front, residual, summed, pos, *refs):
        back = onehot(first, rest, pos[:1, :])
        tail = (dot(back, residual[...]) + summed[...].astype(F32)).astype(BF)
        total = None
        for place, rows in ((onehot(0, first, pos[:1, :]), front[...]), (back, tail)):
            got = lax.dot_general(place, rows, (((0,), (0,)), ((), ())), preferred_element_type=F32)
            total = got if total is None else total + got
        refs[-1][...] = total.astype(BF)

    in_specs = [
        pl.BlockSpec((first, TILE), lambda i: (0, i + skip)),
        pl.BlockSpec((count, TILE), lambda i: (0, i + skip)),
        pl.BlockSpec((rest, TILE), lambda i: (0, i)),
        pl.BlockSpec((RING, count), lambda i: (0, 0)),
    ]
    operands = [front, residual, summed, pos]
    aliases = {}
    if earlier is not None:
        in_specs.append(pl.BlockSpec(memory_space=pl.ANY))
        operands.append(earlier)
        aliases = {4: 0}
    return pl.pallas_call(
        kernel,
        grid=(wide // TILE,),
        in_specs=in_specs,
        out_specs=pl.BlockSpec((count, TILE), lambda i: (0, i + skip)),
        out_shape=jax.ShapeDtypeStruct((count, width), BF),
        input_output_aliases=aliases,
        compiler_params=params(),
        cost_estimate=cost(4 * count * count * wide, 8 * count * wide),
        name="finish_hidden",
    )(*operands)


def dispatch(where, base, recv, gain, pos, placing):
    rows, width = base.shape
    quarter = width // 4
    seats = placing.shape[0]

    half = width // 2

    def kernel(where_ref, base, r0, r1, r2, r3, gain, pos, placing, front, out, held):
        pick = onehot(0, rows, pos[:1, :])
        square = jnp.zeros((rows, 1), F32)
        for n, (a, b) in enumerate(((r0, r2), (r1, r3))):
            at = slice(n * half, (n + 1) * half)
            total = base[:, at] + a[...].astype(F32) + b[...].astype(F32)
            rounded = total.astype(BF)
            front[:, at] = rounded
            total = rounded.astype(F32)
            square = square + jnp.sum(total * total, axis=1, keepdims=True)
        scale = lax.rsqrt(square * (1.0 / width) + 1e-06)
        held[...] = (front[...].astype(F32) * scale * gain[...]).astype(BF)
        seat = lax.dot_general(
            placing[...], pick, (((1,), (1,)), ((), ())), preferred_element_type=F32
        ).astype(BF)
        for side in range(2):
            for n in range(2):
                at = pl.multiple_of((side * 2 + lax.rem(where_ref[1] + n, 2)) * quarter, 128)
                got = dot(seat, held[:, pl.ds(at, quarter)])
                out[side * seats : (side + 1) * seats, n * quarter : (n + 1) * quarter] = got.astype(BF)

    vmem = pl.BlockSpec(memory_space=pltpu.VMEM)
    return pl.pallas_call(
        kernel,
        in_specs=[pl.BlockSpec(memory_space=pltpu.SMEM)] + [vmem] * 8,
        out_specs=[vmem] * 2,
        out_shape=[
            jax.ShapeDtypeStruct((rows, width), BF),
            jax.ShapeDtypeStruct((2 * seats, width // 2), BF),
        ],
        scratch_shapes=[pltpu.VMEM((rows, width), BF)],
        compiler_params=params(),
        cost_estimate=cost(2 * seats * rows * width, 20 * rows * width),
        name="dispatch",
    )(where, base, *recv, gain, pos, placing)


def gate_up(where, blocks, wg, wg2, wu, wu2):
    per = blocks[0][0].shape[0]
    depth, ff = wg.shape
    keep = 2 * per

    def kernel(where_ref, a0, a1, a2, a3, b0, b1, b2, b3, wg, wg2, wu, wu2, mine, away):
        first = jnp.concatenate([a0[...], a1[...], a2[...], a3[...]], axis=0)
        last = jnp.concatenate([b0[...], b1[...], b2[...], b3[...]], axis=0)
        for n, (w, w2) in enumerate(((wg, wg2), (wu, wu2))):
            total = dot(first, w[...]) + dot(last, w2[...])
            columns = slice(n * ff, (n + 1) * ff)
            low = where_ref[3] == 0
            mine[:, columns] = jnp.where(low, total[:keep], total[keep:])
            away[:, columns] = jnp.where(low, total[keep:], total[:keep]).astype(BF)

    vmem = pl.BlockSpec(memory_space=pltpu.VMEM)
    return pl.pallas_call(
        kernel,
        in_specs=[pl.BlockSpec(memory_space=pltpu.SMEM)] + [vmem] * 12,
        out_specs=[vmem, vmem],
        out_shape=[
            jax.ShapeDtypeStruct((keep, 2 * ff), F32),
            jax.ShapeDtypeStruct((keep, 2 * ff), BF),
        ],
        compiler_params=params(),
        cost_estimate=cost(16 * per * 2 * depth * ff, 8 * per * 2 * depth + 8 * depth * ff),
        name="gate_up",
    )(where, *[a for a, _ in blocks], *[b for _, b in blocks], wg, wg2, wu, wu2)


def down(where, mine, other, wd, wd2):
    rows, ff = mine.shape
    quarter = wd.shape[1]
    per = rows // 2

    def kernel(where_ref, mine, other, wd, wd2, *outs):
        low = where_ref[3] == 0
        first = jnp.where(low, mine[...], other[...])
        second = jnp.where(low, other[...], mine[...])
        both = jnp.concatenate([first, second], axis=0)
        for n, w in enumerate((wd, wd2)):
            for c in range(2):
                got = dot(both, w[:, c * TILE : (c + 1) * TILE]).astype(BF)
                for k in range(RING):
                    outs[2 * k + n][:, c * TILE : (c + 1) * TILE] = got[k * per : (k + 1) * per]

    vmem = pl.BlockSpec(memory_space=pltpu.VMEM)
    return pl.pallas_call(
        kernel,
        in_specs=[pl.BlockSpec(memory_space=pltpu.SMEM), vmem, vmem, vmem, vmem],
        out_specs=[vmem] * 8,
        out_shape=[jax.ShapeDtypeStruct((per, quarter), BF)] * 8,
        compiler_params=params(),
        cost_estimate=cost(8 * rows * ff * quarter, 4 * ff * quarter + 8 * rows * quarter),
        name="down",
    )(where, mine, other, wd, wd2)


def mix(where, returned, high, low):
    rows, half = returned.shape
    seats, count = high.shape
    quarter = half // 2

    def kernel(where_ref, returned, high, low, out):
        for side in range(2):
            for n in range(2):
                part = returned[side * seats : (side + 1) * seats, n * quarter : (n + 1) * quarter]
                total = None
                for factor in (high, low):
                    got = lax.dot_general(
                        factor[...], part, (((0,), (0,)), ((), ())), preferred_element_type=F32
                    )
                    total = got if total is None else total + got
                at = pl.multiple_of((2 * side + lax.rem(where_ref[1] + n, 2)) * quarter, 128)
                out[:, pl.ds(at, quarter)] = total.astype(BF)

    vmem = pl.BlockSpec(memory_space=pltpu.VMEM)
    return pl.pallas_call(
        kernel,
        in_specs=[pl.BlockSpec(memory_space=pltpu.SMEM)] + [vmem] * 3,
        out_specs=vmem,
        out_shape=jax.ShapeDtypeStruct((count, 2 * half), BF),
        compiler_params=params(),
        cost_estimate=cost(8 * seats * half * count, 2 * rows * half + 4 * count * half),
        name="mix",
    )(where, returned, high, low)


def find_seats(ids, gates):
    top, count = ids.shape
    seats = EXPERTS * SEAT

    def kernel(ids, gates, placing, high, low):
        row = lax.broadcasted_iota(jnp.int32, (count, count), 0)
        column = lax.broadcasted_iota(jnp.int32, (count, count), 1)
        tri = (row <= column).astype(BF)
        seat = lax.broadcasted_iota(jnp.int32, (SEAT, count), 0)
        for expert in range(EXPERTS):
            match = ids[...] == expert
            here = jnp.sum(match.astype(F32), axis=0, keepdims=True)
            gate = jnp.sum(jnp.where(match, gates[...], 0.0), axis=0, keepdims=True)
            upto = dot(jnp.broadcast_to(here, (SEAT, count)).astype(BF), tri)
            found = (here > 0.0) & (upto == (seat + 1).astype(F32)) & (seat < CAP)
            picked = found.astype(F32)
            factor = picked * gate
            first = factor.astype(BF)
            at = slice(expert * SEAT, (expert + 1) * SEAT)
            placing[at] = picked
            high[at] = first.astype(F32)
            low[at] = factor - first.astype(F32)

    vmem = pl.BlockSpec(memory_space=pltpu.VMEM)
    out = pl.pallas_call(
        kernel,
        in_specs=[vmem, vmem],
        out_specs=[vmem] * 3,
        out_shape=[jax.ShapeDtypeStruct((seats, count), F32)] * 3,
        compiler_params=params(),
        cost_estimate=cost(2 * seats * count * count, 32 * seats * count),
        name="find_seats",
    )(ids, gates)
    return [a.astype(BF) for a in out]


def reseat(rows, columns):
    row = lax.broadcasted_iota(jnp.int32, (rows, columns), 0)
    column = lax.broadcasted_iota(jnp.int32, (rows, columns), 1)
    if rows < columns:
        return ((row // CAP == column // SEAT) & (row % CAP == column % SEAT)).astype(BF)
    return ((row // SEAT == column // CAP) & (row % SEAT == column % CAP)).astype(BF)


def pack(rows):
    wide, half = rows.shape
    short = wide // SEAT * CAP
    quarter = half // 2

    def kernel(rows, first, last):
        take = reseat(short, wide)
        first[...] = dot(take, rows[:, :quarter]).astype(BF)
        last[...] = dot(take, rows[:, quarter:]).astype(BF)

    vmem = pl.BlockSpec(memory_space=pltpu.VMEM)
    return pl.pallas_call(
        kernel,
        in_specs=[vmem],
        out_specs=[vmem, vmem],
        out_shape=[jax.ShapeDtypeStruct((short, quarter), BF)] * 2,
        compiler_params=params(),
        cost_estimate=cost(2 * short * wide * half, 4 * wide * half),
        name="pack",
    )(rows)


def add_parts(own, behind, ahead):
    short, quarter = own[0].shape
    wide = short // CAP * SEAT

    def kernel(*refs):
        put = reseat(wide, short)
        for n in range(2):
            total = refs[n][...].astype(F32) + refs[2 + n][...].astype(F32) + refs[4 + n][...].astype(F32)
            refs[6][:, n * quarter : (n + 1) * quarter] = dot(put, total.astype(BF)).astype(BF)

    vmem = pl.BlockSpec(memory_space=pltpu.VMEM)
    return pl.pallas_call(
        kernel,
        in_specs=[vmem] * 6,
        out_specs=vmem,
        out_shape=jax.ShapeDtypeStruct((wide, 2 * quarter), BF),
        compiler_params=params(),
        cost_estimate=cost(4 * short * wide * quarter, 20 * short * quarter),
        name="add_parts",
    )(*own, *behind, *ahead)


def local(attn_partial, residual, gain, expert_ids, gate_vals, w_gate, w_up, w_down):
    count, width = residual.shape
    ff = w_gate.shape[2]
    barrier = lax.optimization_barrier
    where = jnp.stack([lax.axis_index(a) for a in ("x", "core", "y", "zh")]).astype(jnp.int32)
    grid = ("zh", "y", "zl")
    attn = attn_partial[0]
    wg, wu, wd = w_gate[0], w_up[0], w_down[0]
    gain = gain.reshape(1, width)

    with jax.named_scope("routing"):
        token = jnp.arange(count, dtype=jnp.int32)
        anyone = jnp.any(expert_ids < EXPERTS, axis=1)
        tri = (token[:, None] >= token[None, :]).astype(BF)
        ahead = dot(tri, anyone[:, None].astype(BF)).astype(jnp.int32)[:, 0]
        pos = jnp.where(anyone, ahead - 1, ahead[-1] + token - ahead).reshape(1, count)
        attn = load(attn, pos)
        poses = jnp.concatenate([pos] + [shift(pos, -k) for k in (1, 2, 3)], axis=0)

    with jax.named_scope("weight_swap"):
        wg2 = lax.ppermute(wg, "core", SWAP)
        wu2 = lax.ppermute(wu, "core", SWAP)
        wd2 = lax.ppermute(wd, "core", SWAP)

    back, summed = [], {}

    def head_sum(n, after):
        operand, after = barrier((back[n], after))
        with jax.named_scope("head_sum"):
            summed[n] = lax.psum_scatter(operand, "x", scatter_dimension=0, tiled=True)[0]
        return after

    with jax.named_scope("front_sum"):
        attn, poses = barrier((attn, poses))
        far = select_rows(where, attn, poses, FRONT, (2,))
        far, poses = barrier((far, poses))
        near = select_rows(where, attn, poses, FRONT, (1, 3))
        near, poses, ids, gates = barrier((near, poses, expert_ids.T, gate_vals.T))
        pieces = [tiles * TILE for tiles in PIECES]
        back += back_rows(where, attn, poses, FRONT, 0, pieces[:1])
        seats = find_seats(ids, gates)
        base = own_rows(where, attn, residual, poses, FRONT)
        beside = (back[0], seats, wg2, wu2, wd2)
        behind, ahead, (_, seats, wg2, wu2, wd2) = ring_sum(far, near[:2], near[2:], beside)
        placing, high, low = seats
    with jax.named_scope("rows_out"):
        behind, ahead = head_sum(0, (behind, ahead))
        front, message = dispatch(where, base, (*behind, *ahead), gain, poses, placing)
        late_poses, message = barrier((poses, message))
        back += back_rows(where, attn, late_poses, FRONT, pieces[0], pieces[1:])
        whole = lax.all_to_all(message, grid, split_axis=0, concat_axis=0, tiled=True)
        whole, back[1:] = barrier((whole, back[1:]))
        rows = ring_gather(*pack(whole))
    with jax.named_scope("gate_up"):
        rows = head_sum(1, rows)
        mine, away = gate_up(where, rows, wg, wg2, wu, wu2)
        mine = mine + lax.ppermute(away, "zh", SWAP).astype(F32)
        middle = (jax.nn.silu(mine[:, :ff]) * mine[:, ff:]).astype(BF)
        other = lax.ppermute(middle, "zh", SWAP)
    with jax.named_scope("rows_back"):
        outs = down(where, middle, other, wd, wd2)
        total = add_parts(outs[:2], *ring_sum(outs[4:6], outs[6:8], outs[2:4])[:2])
        total = head_sum(2, total)
        returned = lax.all_to_all(total, grid, split_axis=0, concat_axis=0, tiled=True)
    with jax.named_scope("hidden"):
        hidden = finish_hidden(where, front, residual, summed[0], poses, 0)
        hidden = finish_hidden(where, front, residual, summed[1], poses, pieces[0], hidden)
        returned, hidden = barrier((returned, hidden))
    with jax.named_scope("mix"):
        moe_out = mix(where, returned, high, low)
    with jax.named_scope("hidden"):
        moe_out, hidden = barrier((moe_out, hidden))
        hidden = finish_hidden(where, front, residual, summed[2], poses, sum(pieces[:2]), hidden)
    return hidden, moe_out


def solution(mesh):
    grid = Mesh(mesh.devices.reshape(2, 2, 4, 2, 4), ("zh", "core", "y", "zl", "x"))
    group = ("zh", "core", "y", "zl")
    token = P(group + ("x",), None)
    placed = (
        P("x", group, None),
        token,
        P(),
        token,
        token,
        P(("y", "zl"), ("zh", "core"), "x"),
        P(("y", "zl"), ("zh", "core"), "x"),
        P(("y", "zl"), "x", ("zh", "core")),
    )
    return jax.shard_map(
        local, mesh=grid, in_specs=placed, out_specs=(token, token), check_vma=False
    )
```
